256 devices in a mesh: sub: 64 (over z, y, x_hi), dom: 4 (over x_lo, core).
Axes of the slice: x: 4 (x_hi: 2, x_lo: 2; x = x_hi * 2 + x_lo), y: 4, z: 8, core: 2. Of those that a mesh axis runs over, the one named last changes fastest.
Arguments:
- multipliers: bfloat16 [256, 2048, 128], P('sub', 'dom'), may hold values from -6 to 6
- schur_inverse: bfloat16 [256, 2048, 2048], P('sub', 'dom'), may hold values from -0.125 to 0.125
- corner_coupling: bfloat16 [256, 24, 2048], P('sub', None, 'dom'), may hold values from -0.26367188 to 0.26367188
- coarse_inverse: float32 [4096, 4096], P('dom', 'sub'), may hold values from -0.09375 to 0.09375
- partner: int32 [256, 16], P('sub'), may hold values from 0 to 255, as said below
- corner_map: int32 [256, 24], P('sub'), may hold values from 0 to 4095, as said below
Outputs:
- twice: bfloat16 [256, 2048, 128], P('sub', 'dom')
The draws below stay inside these ranges and needn't reach their ends.
Inputs may be any that keep to these rules, and one draw needn't show every extreme that they name: partner[partner[s, t], t] = s and partner[s, t] != s; the partner lies on the same sub index s // 4, the next or the previous one (cyclically); for each tile slot and sub index at most 2 tiles have a partner on the next sub index and at most 2 on the previous, and both are reached in every draw. `corner_map`: the corners of subdomain s lie in coarse rows (s // 4) * 64 to (s // 4 + 1) * 64 - 1.
All inputs are finite; a program needn't handle non-finite values.
Results may differ from the reference program's by a relative error of at most 0.0055.
Values may be sent and summed in bfloat16 or wider, within the bound.
No kernel may reach another device: no remote copies, remote signals or barrier semaphores. Data moves between devices by JAX's collectives and lax.ppermute only.
A program may use at most 64 MiB of HBM per device.

```python
import jax
import jax.numpy as jnp
from jax import lax

SUB_DEV = 4
NSUB = 256
NIF = 2048
TILE = 128
NTILE = 16
RHS = 128
NCORN = 24
COARSE_DEV = 64
NCOARSE = 4096


def draw_partner(key, part):
    key = jax.random.fold_in(key, 11)
    devices = NSUB // SUB_DEV
    slots = NIF // TILE
    key_mode, key_even, key_order = jax.random.split(key, 3)
    slot_ids = jnp.arange(slots, dtype=jnp.int32)
    device_ids = jnp.arange(devices, dtype=jnp.int32)
    odd_mode = jax.random.randint(key_mode, (slots,), 0, 2, dtype=jnp.int32)
    odd_mode = jnp.where(slot_ids < 2, 0, odd_mode)
    even_cross = 2 * jax.random.randint(key_even, (slots, devices), 0, 2, dtype=jnp.int32)
    forced = (slot_ids[:, None] < 2) & (device_ids[None, :] == 0)
    even_cross = jnp.where(forced, 2, even_cross)
    crossing = jnp.where(odd_mode[:, None] == 1, 1, even_cross)
    scores = jax.random.randint(key_order, (slots, devices, SUB_DEV), 0, 1 << 20, dtype=jnp.int32)
    scores = scores * SUB_DEV + jnp.arange(SUB_DEV, dtype=jnp.int32)
    placed = jnp.argsort(scores, axis=-1).astype(jnp.int32)
    position = jnp.argsort(placed, axis=-1).astype(jnp.int32)
    left_count = crossing[:, (device_ids - 1) % devices][:, :, None]
    right_count = crossing[:, :, None]
    goes_left = position < left_count
    goes_right = position >= SUB_DEV - right_count
    here = device_ids[None, :, None]
    other_device = jnp.where(goes_left, (here - 1) % devices, jnp.where(goes_right, (here + 1) % devices, here))
    middle = left_count + jnp.bitwise_xor(position - left_count, 1)
    other_position = jnp.where(goes_left, SUB_DEV - left_count + position, jnp.where(goes_right, position - (SUB_DEV - right_count), middle))
    slot_index = slot_ids[:, None, None]
    other_local = placed[slot_index, other_device, other_position]
    result = SUB_DEV * other_device + other_local
    return jnp.transpose(result, (1, 2, 0)).reshape(NSUB, slots).astype(jnp.int32)


def draw_corner_map(key, part):
    key = jax.random.fold_in(key, 13)
    local_rows = jax.random.randint(key, (NSUB, NCORN), 0, COARSE_DEV, dtype=jnp.int32)
    subdomain_ids = jnp.arange(NSUB, dtype=jnp.int32)[:, None]
    corner_ids = jnp.arange(NCORN, dtype=jnp.int32)[None, :]
    local_rows = jnp.where((subdomain_ids == NSUB - 1) & (corner_ids == 0), COARSE_DEV - 1, local_rows)
    local_rows = jnp.where((subdomain_ids == 0) & (corner_ids == 0), 0, local_rows)
    return (subdomain_ids // SUB_DEV * COARSE_DEV + local_rows).astype(jnp.int32)


def levels(rng, extent, cuts, least, largest):
    def one(dim, shards_of):
        heights = jax.random.uniform(jax.random.fold_in(jax.random.fold_in(rng, 6), dim), (shards_of,), jnp.float32, least / len(cuts), largest / len(cuts))
        return jnp.repeat(jnp.exp(heights), extent[dim] // shards_of).reshape((-1,) + (1,) * (len(extent) - dim - 1))

    factor_of = one(*cuts[0])
    for cut in cuts[1:]:
        factor_of = factor_of * one(*cut)
    return factor_of


def scatter_about(rng, dims, deviation, bound, cuts=(), kind=jnp.bfloat16):
    values = deviation * jax.random.normal(rng, dims, jnp.float32)
    if cuts:
        values = values * levels(rng, dims, cuts, -0.22, 0.18)
    return jnp.clip(values, -bound, bound).astype(kind)


def setup_inputs(seed: int = 0) -> dict:
    keys = jax.random.split(jax.random.key(seed), 7)
    multipliers = scatter_about(keys[0], (NSUB, NIF, RHS), 1.0, 6.0, ((0, 64), (1, 4)))
    schur_inverse = scatter_about(keys[1], (NSUB, NIF, NIF), NIF ** -0.5, 0.125, ((0, 64), (1, 4)))
    corner_coupling = scatter_about(keys[2], (NSUB, NCORN, NIF), (2.0 / NIF ** 0.5), 0.26367188, ((0, 64), (2, 4)))
    coarse_inverse = scatter_about(keys[3], (NCOARSE, NCOARSE), NCOARSE ** -0.5, 0.09375, ((0, 4), (1, 64)), jnp.float32)
    partner = draw_partner(jax.random.fold_in(keys[6], 71), 0)
    corner_map = draw_corner_map(jax.random.fold_in(keys[6], 71), 0)
    return dict(multipliers=multipliers, schur_inverse=schur_inverse, corner_coupling=corner_coupling, coarse_inverse=coarse_inverse, partner=partner, corner_map=corner_map)


def apply_once(values, schur_inverse, corner_coupling, coarse_inverse, partner, corner_map, signs):
    sign_rows = jnp.repeat(signs, TILE, axis=1)[:, :, None]
    signed = (values.astype(jnp.float32) * sign_rows).astype(jnp.bfloat16)

    def one_product(pair):
        return jnp.dot(pair[0], pair[1], preferred_element_type=jnp.float32)

    direct = lax.map(one_product, (schur_inverse, signed))
    coupling_wide = corner_coupling.astype(jnp.float32)
    corner_part = jnp.einsum('sjn,snr->sjr', coupling_wide, signed.astype(jnp.float32), precision=lax.Precision.HIGHEST)
    coarse_load = jnp.zeros((NCOARSE, RHS), jnp.float32).at[corner_map.reshape(-1)].add(corner_part.reshape(-1, RHS))
    coarse = jnp.dot(coarse_inverse, coarse_load, precision=lax.Precision.HIGHEST)
    corner_values = coarse[corner_map.reshape(-1)].reshape(NSUB, NCORN, RHS)
    back = jnp.einsum('sjn,sjr->snr', coupling_wide, corner_values, precision=lax.Precision.HIGHEST)
    solved = (direct + back).astype(jnp.bfloat16)
    tiles = solved.reshape(NSUB, NTILE, TILE, RHS)
    slot_ids = jnp.arange(NTILE, dtype=jnp.int32)[None, :]
    partner_tiles = tiles[partner, slot_ids]
    result = signs[:, :, None, None] * (tiles.astype(jnp.float32) - partner_tiles.astype(jnp.float32))
    return result.astype(jnp.bfloat16).reshape(NSUB, NIF, RHS)


def reference(multipliers, schur_inverse, corner_coupling, coarse_inverse, partner, corner_map):
    owners = jnp.arange(NSUB, dtype=jnp.int32)[:, None]
    signs = jnp.where(owners < partner, 1.0, -1.0).astype(jnp.float32)
    first = apply_once(multipliers, schur_inverse, corner_coupling, coarse_inverse, partner, corner_map, signs)
    return apply_once(first, schur_inverse, corner_coupling, coarse_inverse, partner, corner_map, signs)
```

```python
import functools

import jax
import jax.numpy as jnp
from jax import lax
from jax.experimental import pallas as pl
from jax.experimental.pallas import tpu as pltpu
from jax.sharding import PartitionSpec as P

TILE = 128
F32 = jnp.float32
BF16 = jnp.bfloat16
SMEM = pltpu.SMEM
VMEM_BYTES = 40 * 1024 * 1024


def shifted(block, axis, distance):
    n = lax.axis_size(axis)
    return lax.ppermute(block, axis, [(i, (i + distance) % n) for i in range(n)])


def swapped(block, axis, mask):
    n = lax.axis_size(axis)
    return lax.ppermute(block, axis, [(i, i ^ mask) for i in range(n)])


def halves(x):
    high = lax.reduce_precision(x, 8, 7)
    return high.astype(BF16), (x - high).astype(BF16)


def dot(a, b, dims=((1,), (0,)), precision=None):
    return lax.dot_general(a, b, (dims, ((), ())), precision=precision, preferred_element_type=F32)


def product_kernel(slots, with_coupling, order, after, before, s_ref, u0, u1, u2, u3, *refs):
    if with_coupling:
        coupling, direct_ref, to_after, to_before = refs
    else:
        direct_ref, to_after, to_before = refs
    step = pl.program_id(0)
    depth = u0.shape[1]

    @pl.when(step == 0)
    def _():
        to_after[...] = jnp.zeros_like(to_after)
        to_before[...] = jnp.zeros_like(to_before)

    total = None
    for place, piece in enumerate((u0, u1, u2, u3)):
        columns = pl.ds(pl.multiple_of(order[place] * depth, depth), depth)
        term = dot(s_ref[0, :, columns], piece[0])
        total = term if total is None else total + term
    direct_ref[...] = total.reshape(direct_ref.shape)
    for t in range(slots):
        for index, target in ((after, to_after), (before, to_before)):
            place = index[step * slots + t]

            @pl.when(place >= 0)
            def _(t=t, place=place, target=target):
                tile = total[t * TILE : (t + 1) * TILE]
                target[pl.ds(place, 1), :TILE] = tile.astype(BF16)[None]
                if with_coupling:
                    target[pl.ds(place, 1), TILE:] = coupling[pl.ds(t, 1)]


def product(schur_inverse, pieces, order, after, before, coupling_tiles):
    sub_dev, rows, cols = schur_inverse.shape
    depth, rhs = pieces[0].shape[1:]
    slots = rows // TILE
    extra = 0 if coupling_tiles is None else coupling_tiles.shape[1]
    packed = jax.ShapeDtypeStruct((2 * slots, TILE + extra, rhs), BF16)
    whole = pl.BlockSpec(packed.shape, lambda i: (0, 0, 0))
    operands = [order, after, before, schur_inverse, *pieces]
    in_specs = [pl.BlockSpec(memory_space=SMEM)] * 3
    in_specs += [pl.BlockSpec((1, rows, cols), lambda i: (i, 0, 0))]
    in_specs += [pl.BlockSpec((1, depth, rhs), lambda i: (i, 0, 0))] * 4
    if extra:
        operands.append(coupling_tiles)
        in_specs.append(pl.BlockSpec((slots, extra, TILE), lambda i: (i, 0, 0)))
    return pl.pallas_call(
        functools.partial(product_kernel, slots, bool(extra)),
        grid=(sub_dev,),
        in_specs=in_specs,
        out_specs=[pl.BlockSpec((slots, TILE, rhs), lambda i: (i, 0, 0)), whole, whole],
        out_shape=[jax.ShapeDtypeStruct((sub_dev * slots, TILE, rhs), F32), packed, packed],
        compiler_params=pltpu.CompilerParams(vmem_limit_bytes=VMEM_BYTES),
        cost_estimate=pl.CostEstimate(
            flops=2 * sub_dev * rows * cols * rhs, bytes_accessed=2 * sub_dev * rows * cols, transcendentals=0
        ),
    )(*operands)


def difference_kernel(kind, index, direct, from_before, from_after, coupling, delta, spread, load):
    n_tiles, dofs = coupling.shape[:2]
    rhs = direct.shape[2]
    total = None
    for p in range(n_tiles):
        mine = coupling[p].astype(F32)
        blank = jnp.zeros((dofs, TILE), BF16)
        where, which = kind[p], index[p]

        @pl.when(where == 0)
        def _(p=p, which=which, mine=mine, blank=blank):
            delta[p] = direct[p] - direct[which]
            other = mine - coupling[which].astype(F32)
            spread[p] = jnp.concatenate([blank, other.astype(BF16), blank], axis=0)

        @pl.when(where == 1)
        def _(p=p, which=which, blank=blank):
            delta[p] = direct[p] - from_after[which, :TILE].astype(F32)
            spread[p] = jnp.concatenate([blank, coupling[p], -from_after[which, TILE:]], axis=0)

        @pl.when(where == 2)
        def _(p=p, which=which, blank=blank):
            delta[p] = direct[p] - from_before[which, :TILE].astype(F32)
            spread[p] = jnp.concatenate([-from_before[which, TILE:], coupling[p], blank], axis=0)

        first = dot(coupling[p], delta[p].astype(BF16))
        second = dot(coupling[p], spread[p], ((1,), (1,)))
        part = jnp.concatenate([first, second], axis=1)
        total = part if total is None else total + part
    load[...] = total


def difference(kind, index, direct, from_before, from_after, coupling):
    n_tiles, dofs, _ = coupling.shape
    rhs = direct.shape[2]
    vmem = pl.BlockSpec(memory_space=pltpu.VMEM)
    return pl.pallas_call(
        difference_kernel,
        in_specs=[pl.BlockSpec(memory_space=SMEM)] * 2 + [vmem] * 4,
        out_specs=[vmem] * 3,
        out_shape=[
            jax.ShapeDtypeStruct((n_tiles, TILE, rhs), F32),
            jax.ShapeDtypeStruct((n_tiles, 3 * dofs, TILE), BF16),
            jax.ShapeDtypeStruct((dofs, rhs + 3 * dofs), F32),
        ],
        compiler_params=pltpu.CompilerParams(vmem_limit_bytes=VMEM_BYTES),
        cost_estimate=pl.CostEstimate(flops=10**8, bytes_accessed=3 * 10**6, transcendentals=0),
    )(kind, index, direct, from_before, from_after, coupling)


def split(x):
    high = x.astype(BF16)
    return high, (x - high.astype(F32)).astype(BF16)


def applied(spread, high, low):
    return dot(spread, high, ((0,), (0,))) + dot(spread, low, ((0,), (0,)))


def next_kernel(coarse_parts, load_parts, delta, spread, u_ref, load_ref):
    coarse = (coarse_parts[0] + coarse_parts[1]) + (coarse_parts[2] + coarse_parts[3])
    high, low = split(coarse)
    rhs = coarse.shape[1]
    load = (load_parts[0] + load_parts[1]) + (load_parts[2] + load_parts[3])
    load = load[:, :rhs] + dot(load[:, rhs:], coarse, precision=lax.Precision.HIGHEST)
    load_ref[...] = load.astype(BF16)
    for p in range(delta.shape[0]):
        u_ref[p] = (delta[p] + applied(spread[p], high, low)).astype(BF16)


def next_values(coarse_parts, load_parts, delta, spread):
    vmem = pl.BlockSpec(memory_space=pltpu.VMEM)
    return pl.pallas_call(
        next_kernel,
        in_specs=[vmem] * 4,
        out_specs=[vmem] * 2,
        out_shape=[
            jax.ShapeDtypeStruct(delta.shape, BF16),
            jax.ShapeDtypeStruct((load_parts.shape[1], delta.shape[2]), BF16),
        ],
        compiler_params=pltpu.CompilerParams(vmem_limit_bytes=VMEM_BYTES),
        cost_estimate=pl.CostEstimate(flops=10**8, bytes_accessed=3 * 10**6, transcendentals=0),
    )(coarse_parts, load_parts, delta, spread)


def last_kernel(kind, index, signs, coarse_parts, direct, from_before, from_after, spread, out):
    coarse = (coarse_parts[0] + coarse_parts[1]) + (coarse_parts[2] + coarse_parts[3])
    high, low = split(coarse)
    for p in range(direct.shape[0]):
        where, which = kind[p], index[p]
        base = direct[p] + applied(spread[p], high, low)

        @pl.when(where == 0)
        def _(p=p, which=which, base=base):
            out[p] = (signs[p] * (base - direct[which])).astype(BF16)

        @pl.when(where == 1)
        def _(p=p, which=which, base=base):
            out[p] = (signs[p] * (base - from_after[which].astype(F32))).astype(BF16)

        @pl.when(where == 2)
        def _(p=p, which=which, base=base):
            out[p] = (signs[p] * (base - from_before[which].astype(F32))).astype(BF16)


def last_values(kind, index, signs, coarse_parts, direct, from_before, from_after, spread):
    vmem = pl.BlockSpec(memory_space=pltpu.VMEM)
    return pl.pallas_call(
        last_kernel,
        in_specs=[pl.BlockSpec(memory_space=SMEM)] * 3 + [vmem] * 5,
        out_specs=vmem,
        out_shape=jax.ShapeDtypeStruct(direct.shape, BF16),
        compiler_params=pltpu.CompilerParams(vmem_limit_bytes=VMEM_BYTES),
        cost_estimate=pl.CostEstimate(flops=10**8, bytes_accessed=3 * 10**6, transcendentals=0),
    )(kind, index, signs, coarse_parts, direct, from_before, from_after, spread)


def body(multipliers, schur_inverse, corner_coupling, coarse_inverse, partner, corner_map):
    n_sub = lax.axis_size("sub")
    n_dom = lax.axis_size("dom")
    sub = lax.axis_index("sub")
    dom = lax.axis_index("dom")
    sub_dev, block_rows, rhs = multipliers.shape
    slots = block_rows // TILE
    n_tiles = sub_dev * slots
    coarse_block, coarse_dev = coarse_inverse.shape
    share = coarse_dev // n_dom

    partners = lax.dynamic_slice_in_dim(partner, dom * slots, slots, 1)
    ids = sub * sub_dev + jnp.arange(sub_dev, dtype=jnp.int32)
    signs = jnp.where(ids[:, None] < partners, 1.0, -1.0).astype(F32)
    sign_rows = jnp.repeat(signs, TILE, axis=1)[:, :, None]
    local = partners % sub_dev
    relation = (partners // sub_dev - sub) % n_sub
    kind = jnp.where(relation == 0, 0, jnp.where(relation == 1, 1, 2)).astype(jnp.int32)
    slot_ids = jnp.arange(slots, dtype=jnp.int32)[None]
    same_kind = kind[None] == kind[:, None]
    subs = jnp.arange(sub_dev, dtype=jnp.int32)
    earlier = same_kind & (subs[None] < subs[:, None])[:, :, None]
    lower = same_kind & (local[None] < local[:, None])
    sent = jnp.sum(earlier.astype(jnp.int32), axis=1) * slots + slot_ids
    got = jnp.sum(lower.astype(jnp.int32), axis=1) * slots + slot_ids
    after = jnp.where(kind == 1, sent, -1).reshape(-1)
    before = jnp.where(kind == 2, sent, -1).reshape(-1)
    index = jnp.where(kind == 0, local * slots + slot_ids, got).reshape(-1)
    kind = kind.reshape(-1)
    order = dom ^ jnp.arange(n_dom, dtype=jnp.int32)

    corner_local = corner_map - sub * coarse_dev
    corner_table = (
        corner_local[:, :, None] == jnp.arange(coarse_dev, dtype=jnp.int32)[None, None]
    ).astype(BF16)
    coupling = jnp.einsum(
        "sjk,sjn->skn", corner_table, corner_coupling, preferred_element_type=F32
    ).astype(BF16)
    coupling_tiles = (
        coupling.reshape(sub_dev, coarse_dev, slots, TILE)
        .transpose(0, 2, 1, 3)
        .reshape(n_tiles, coarse_dev, TILE)
    )

    def gathered(u):
        far = swapped(u, "dom", 2)
        return u, swapped(u, "dom", 1), far, swapped(far, "dom", 1)

    def coarse_parts(k_rows, load_rows):
        part = jnp.einsum("kr,kx->rx", k_rows, load_rows, preferred_element_type=F32)
        return lax.all_gather(part, "dom", axis=0)

    u1 = (multipliers.astype(F32) * sign_rows).astype(BF16)
    pieces1 = gathered(u1)
    high, low = halves(jnp.einsum("skn,snr->kr", coupling, u1, preferred_element_type=F32))
    inverse_t = coarse_inverse.T.astype(BF16)
    to_dom = jnp.concatenate([inverse_t, high, low], axis=1)
    by_dom = lax.all_to_all(to_dom, "dom", 0, 0, tiled=True).reshape(n_dom, share, -1)
    load1 = jnp.sum(by_dom[:, :, coarse_block:].astype(F32), axis=0)
    load1 = (load1[:, :rhs] + load1[:, rhs:]).astype(BF16)
    blocks = by_dom[:, :, :coarse_block].reshape(n_dom, share, -1, 2 * coarse_dev)
    blocks = blocks.transpose(0, 2, 1, 3).reshape(-1, share, 2 * coarse_dev)
    twice_each = jnp.repeat(blocks, 2, axis=0)
    to_sub = jnp.stack(
        [
            jnp.roll(twice_each, 1, axis=0),
            jnp.roll(twice_each, -1, axis=0),
            jnp.broadcast_to(load1[None], (n_sub, share, rhs)),
        ],
        axis=1,
    )
    by_sub = lax.all_to_all(to_sub, "sub", 0, 0, tiled=True)
    direct1, to_after, to_before = product(
        schur_inverse, pieces1, order, after, before, coupling_tiles
    )
    got_before, got_after = shifted(to_after, "sub", 1), shifted(to_before, "sub", -1)
    by_sub, direct1 = lax.optimization_barrier((by_sub, direct1))
    k_wide = jnp.concatenate([by_sub[:, 0], by_sub[:, 1]], axis=2).reshape(n_sub * share, -1)
    offset = jnp.where(sub % 2 == 0, coarse_dev, 0)
    k_rows = lax.dynamic_slice_in_dim(k_wide, offset, 3 * coarse_dev, 1)
    coarse1 = coarse_parts(k_rows, by_sub[:, 2].reshape(n_sub * share, rhs))
    delta1, spread, load2 = difference(
        kind, index, direct1, got_before, got_after, coupling_tiles
    )
    load2 = lax.all_to_all(load2, "dom", 0, 0, tiled=True).reshape(n_dom, share, -1)

    u2, load2 = next_values(coarse1, load2, delta1, spread)
    pieces2 = gathered(u2.reshape(sub_dev, block_rows, rhs))
    by_sub2 = lax.all_to_all(
        jnp.broadcast_to(load2[None], (n_sub, share, rhs)), "sub", 0, 0, tiled=True
    )
    direct2, to_after2, to_before2 = product(
        schur_inverse, pieces2, order, after, before, None
    )
    got_before2, got_after2 = shifted(to_after2, "sub", 1), shifted(to_before2, "sub", -1)
    by_sub2, direct2 = lax.optimization_barrier((by_sub2, direct2))
    coarse2 = coarse_parts(k_rows, by_sub2.reshape(n_sub * share, rhs))
    result = last_values(
        kind, index, signs.reshape(-1), coarse2, direct2, got_before2, got_after2, spread
    )
    return result.reshape(sub_dev, block_rows, rhs)


def solution(mesh):
    placed = (
        P("sub", "dom", None),
        P("sub", "dom", None),
        P("sub", None, "dom"),
        P("dom", "sub"),
        P("sub", None),
        P("sub", None),
    )
    return jax.shard_map(
        body, mesh=mesh, in_specs=placed, out_specs=P("sub", "dom", None), check_vma=False
    )
```

```python
import functools

import jax
import jax.numpy as jnp
from jax import lax
from jax.experimental import pallas as pl
from jax.experimental.pallas import tpu as pltpu
from jax.sharding import PartitionSpec as P

TILE = 128
F32 = jnp.float32
BF16 = jnp.bfloat16
VMEM_BYTES = 24 * 1024 * 1024
MOST_VMEM_BYTES = 59 * 1024 * 1024
IN_SMEM = pl.BlockSpec(memory_space=pltpu.SMEM)
IN_VMEM = pl.BlockSpec(memory_space=pltpu.VMEM)


def like(shape, dtype):
    return jax.ShapeDtypeStruct(shape, dtype)


def params(limit=VMEM_BYTES):
    return pltpu.CompilerParams(vmem_limit_bytes=limit)


def cost(flops, moved):
    return pl.CostEstimate(flops=flops, bytes_accessed=moved, transcendentals=0)


def shifted(block, axis, distance):
    n = lax.axis_size(axis)
    return lax.ppermute(block, axis, [(i, (i + distance) % n) for i in range(n)])


def swapped(block, axis, mask):
    n = lax.axis_size(axis)
    return lax.ppermute(block, axis, [(i, i ^ mask) for i in range(n)])


def dot(a, b, dims=((1,), (0,))):
    return lax.dot_general(a, b, (dims, ((), ())), preferred_element_type=F32)


def split(x):
    high = x.astype(BF16)
    return high, (x - high.astype(F32)).astype(BF16)


def exact_dot(a, b):
    a_high, a_low = split(a)
    b_high, b_low = split(b)
    return dot(a_high, b_high) + (dot(a_high, b_low) + dot(a_low, b_high))


def applied(spread, high, low):
    return dot(spread, high, ((0,), (0,))) + dot(spread, low, ((0,), (0,)))


def partial_rows(got, load, part):
    height, half = got.shape[2], load.shape[0]
    for d in range(got.shape[0]):
        for h in range(2):
            at = (2 * d + h) * height
            block = got[d, :height, h * half : (h + 1) * half]
            part[at : at + height] = exact_dot(block, load).astype(BF16)


def first_kernel(got, part):
    height = got.shape[2]
    load = (got[0, height:] + got[1, height:]) + (got[2, height:] + got[3, height:])
    partial_rows(got, load, part)


def first_part(got):
    rows = 2 * got.shape[0] * got.shape[2]
    return pl.pallas_call(
        first_kernel,
        in_specs=[IN_VMEM],
        out_specs=IN_VMEM,
        out_shape=like((rows, got.shape[2]), BF16),
        compiler_params=params(),
        cost_estimate=cost(10**7, 10**6),
    )(got)


def pack_tiles(after, before, to_after, to_before, tile_at):
    sub_dev, slots = after.shape
    to_after[...] = jnp.zeros_like(to_after)
    to_before[...] = jnp.zeros_like(to_before)
    for i in range(sub_dev):
        for t in range(slots):
            for table, target in ((after, to_after), (before, to_before)):
                place = table[i, t]

                @pl.when(place >= 0)
                def _(i=i, t=t, place=place, target=target):
                    target[pl.ds(place, 1)] = tile_at(i, t).astype(BF16)[None]


def pack_kernel(after, before, coupling, to_after, to_before):
    def tile_at(i, t):
        return coupling[i, :, t * TILE : (t + 1) * TILE]

    pack_tiles(after, before, to_after, to_before, tile_at)


def packed_coupling(after, before, coupling):
    packed = like((2 * after.shape[1], coupling.shape[1], TILE), BF16)
    return pl.pallas_call(
        pack_kernel,
        in_specs=[IN_SMEM] * 2 + [IN_VMEM],
        out_specs=[IN_VMEM] * 2,
        out_shape=[packed, packed],
        compiler_params=params(),
        cost_estimate=cost(10**5, 10**6),
    )(after, before, coupling)


def product_kernel(first, *refs):
    if first:
        after, before, signs, s_ref, u0, u1, u2, u3, direct_ref, to_after, to_before = refs
    else:
        s_ref, u0, u1, u2, u3, direct_ref = refs
    depth, rhs = u0.shape[1:]
    slots = direct_ref.shape[0]
    dom = lax.axis_index("dom")
    step = pl.program_id(0)
    total = None
    for m, piece in enumerate((u0, u1, u2, u3)):
        place = dom ^ m
        values = piece[0]
        if first:
            values = jnp.concatenate(
                [
                    (values[t * TILE : (t + 1) * TILE].astype(F32) * signs[step, place * slots + t]).astype(
                        BF16
                    )
                    for t in range(slots)
                ],
                axis=0,
            )
        columns = pl.ds(pl.multiple_of(place * depth, depth), depth)
        term = dot(s_ref[0, :, columns], values)
        total = term if total is None else total + term
    direct_ref[...] = total.reshape(slots, TILE, rhs)
    if first:

        @pl.when(step == 0)
        def _():
            to_after[...] = jnp.zeros_like(to_after)
            to_before[...] = jnp.zeros_like(to_before)

        for t in range(slots):
            for table, target in ((after, to_after), (before, to_before)):
                place = table[step, t]

                @pl.when(place >= 0)
                def _(t=t, place=place, target=target):
                    target[pl.ds(place, 1)] = direct_ref[pl.ds(t, 1)].astype(BF16)


def product(schur_inverse, pieces, tables=()):
    sub_dev, rows, cols = schur_inverse.shape
    depth, rhs = pieces[0].shape[1:]
    slots = rows // TILE
    first = bool(tables)
    out_shape = [like((sub_dev * slots, TILE, rhs), F32)]
    out_specs = [pl.BlockSpec((slots, TILE, rhs), lambda i: (i, 0, 0))]
    if first:
        packed = (2 * slots, TILE, rhs)
        out_shape += [like(packed, BF16)] * 2
        out_specs += [pl.BlockSpec(packed, lambda i: (0, 0, 0))] * 2
    return pl.pallas_call(
        functools.partial(product_kernel, first),
        grid=(sub_dev,),
        in_specs=[IN_SMEM] * len(tables)
        + [pl.BlockSpec((1, rows, cols), lambda i: (i, 0, 0))]
        + [pl.BlockSpec((1, depth, rhs), lambda i: (i, 0, 0))] * len(pieces),
        out_specs=out_specs,
        out_shape=out_shape,
        compiler_params=params(MOST_VMEM_BYTES),
        cost_estimate=cost(2 * sub_dev * rows * cols * rhs, 2 * sub_dev * rows * cols),
    )(*tables, schur_inverse, *pieces)


def weighted_kernel(after, before, r0, r1, r2, r3, direct, coupling, w_ref, to_after, to_before, coarse):
    share = r0.shape[0]
    dom = lax.axis_index("dom")
    for m, rows in enumerate((r0, r1, r2, r3)):
        coarse[pl.ds(pl.multiple_of((dom ^ m) * share, share), share)] = rows[...]
    high, low = split(coarse[...])
    sub_dev = coupling.shape[0]
    slots = direct.shape[0] // sub_dev
    for i in range(sub_dev):
        for t in range(slots):
            own = coupling[i, :, t * TILE : (t + 1) * TILE]
            w_ref[i * slots + t] = (direct[i * slots + t] + applied(own, high, low)).astype(BF16)
    pack_tiles(after, before, to_after, to_before, lambda i, t: w_ref[i * slots + t])


def weighted(after, before, rows, direct, coupling):
    rhs = direct.shape[2]
    packed = (2 * after.shape[1], TILE, rhs)
    return pl.pallas_call(
        weighted_kernel,
        in_specs=[IN_SMEM] * 2 + [IN_VMEM] * 6,
        out_specs=[IN_VMEM] * 3,
        out_shape=[like(direct.shape, BF16), like(packed, BF16), like(packed, BF16)],
        scratch_shapes=[pltpu.VMEM((4 * rows[0].shape[0], rhs), F32)],
        compiler_params=params(),
        cost_estimate=cost(10**8, 3 * 10**6),
    )(after, before, *rows, direct, coupling)


def spread_kernel(kind, index, coupling, from_before, from_after, spread, second):
    sub_dev, dofs, _ = coupling.shape
    slots = kind.shape[1]
    blank = jnp.zeros((dofs, TILE), BF16)
    total = None
    for i in range(sub_dev):
        for t in range(slots):
            p = i * slots + t
            columns = slice(t * TILE, (t + 1) * TILE)
            mine = coupling[i, :, columns]
            where, which = kind[i, t], index[i, t]
            spread[p, :dofs] = blank
            spread[p, dofs : 2 * dofs] = mine
            spread[p, 2 * dofs :] = blank

            @pl.when(where == 0)
            def _(p=p, i=i, which=which, columns=columns):
                other = coupling[i, :, columns].astype(F32) - coupling[which, :, columns].astype(F32)
                spread[p, dofs : 2 * dofs] = other.astype(BF16)

            @pl.when(where == 1)
            def _(p=p, which=which):
                spread[p, 2 * dofs :] = -from_after[which]

            @pl.when(where == 2)
            def _(p=p, which=which):
                spread[p, :dofs] = -from_before[which]

            term = dot(mine, spread[p], ((1,), (1,)))
            total = term if total is None else total + term
    second[:dofs] = total[:, :TILE]
    second[dofs:] = jnp.concatenate([total[:, TILE:], jnp.zeros_like(total[:, TILE:])], axis=1)


def spread_of(kind, index, coupling, from_before, from_after):
    sub_dev, dofs, cols = coupling.shape
    n_tiles = sub_dev * cols // TILE
    return pl.pallas_call(
        spread_kernel,
        in_specs=[IN_SMEM] * 2 + [IN_VMEM] * 3,
        out_specs=[IN_VMEM] * 2,
        out_shape=[like((n_tiles, 3 * dofs, TILE), BF16), like((2 * dofs, TILE), F32)],
        compiler_params=params(),
        cost_estimate=cost(10**8, 2 * 10**6),
    )(kind, index, coupling, from_before, from_after)


def difference_kernel(
    kind, index, r0, r1, r2, direct, from_before, from_after, coupling, second, delta, sent
):
    sub_dev, dofs, _ = coupling.shape
    slots = kind.shape[1]
    share = r0.shape[0]
    for b, rows in enumerate((r0, r1, r2)):
        sent[b * share : (b + 1) * share] = rows[...]
    at = 3 * share
    sent[at + dofs :] = second[...]
    total = None
    for i in range(sub_dev):
        for t in range(slots):
            p = i * slots + t
            where, which = kind[i, t], index[i, t]

            @pl.when(where == 0)
            def _(p=p, t=t, which=which):
                delta[p] = direct[p] - direct[which * slots + t]

            @pl.when(where == 1)
            def _(p=p, which=which):
                delta[p] = direct[p] - from_after[which].astype(F32)

            @pl.when(where == 2)
            def _(p=p, which=which):
                delta[p] = direct[p] - from_before[which].astype(F32)

            term = dot(coupling[i, :, t * TILE : (t + 1) * TILE], delta[p].astype(BF16))
            total = term if total is None else total + term
    sent[at : at + dofs] = total


def difference(kind, index, rows, direct, from_before, from_after, coupling, second):
    rhs = direct.shape[2]
    dofs = coupling.shape[1]
    return pl.pallas_call(
        difference_kernel,
        in_specs=[IN_SMEM] * 2 + [IN_VMEM] * 8,
        out_specs=[IN_VMEM] * 2,
        out_shape=[
            like(direct.shape, F32),
            like((3 * rows[0].shape[0] + dofs + second.shape[0], rhs), F32),
        ],
        compiler_params=params(),
        cost_estimate=cost(10**8, 3 * 10**6),
    )(kind, index, *rows, direct, from_before, from_after, coupling, second)


def coarse_rows(got, share):
    return jnp.concatenate(
        [got[d, b * share : (b + 1) * share] for b in range(3) for d in range(got.shape[0])], axis=0
    )


def next_kernel(share, dofs, got, delta, spread, inverse, u_ref, part):
    coarse = coarse_rows(got, share)
    at = 3 * share
    total = (got[0, at:] + got[1, at:]) + (got[2, at:] + got[3, at:])
    load = total[:dofs] + exact_dot(total[dofs : 2 * dofs], coarse[:TILE])
    load = load + exact_dot(total[2 * dofs :, : 3 * dofs - TILE], coarse[TILE:])
    partial_rows(inverse, load, part)
    high, low = split(coarse)
    for p in range(delta.shape[0]):
        u_ref[p] = (delta[p] + applied(spread[p], high, low)).astype(BF16)


def next_values(got, delta, spread, inverse, share):
    dofs = spread.shape[1] // 3
    rhs = delta.shape[2]
    part = (2 * inverse.shape[0] * inverse.shape[2], rhs)
    return pl.pallas_call(
        functools.partial(next_kernel, share, dofs),
        in_specs=[IN_VMEM] * 4,
        out_specs=[IN_VMEM] * 2,
        out_shape=[like(delta.shape, BF16), like(part, BF16)],
        compiler_params=params(),
        cost_estimate=cost(10**8, 3 * 10**6),
    )(got, delta, spread, inverse)


def last_kernel(kind, index, signs, w, from_before, from_after, out):
    sub_dev, slots = kind.shape
    for i in range(sub_dev):
        for t in range(slots):
            p = i * slots + t
            where, which = kind[i, t], index[i, t]

            def put(tile, p=p, i=i, t=t):
                out[p] = (signs[i, t] * (w[p].astype(F32) - tile.astype(F32))).astype(BF16)

            @pl.when(where == 0)
            def _(put=put, which=which, t=t):
                put(w[which * slots + t])

            @pl.when(where == 1)
            def _(put=put, which=which):
                put(from_after[which])

            @pl.when(where == 2)
            def _(put=put, which=which):
                put(from_before[which])


def last_values(kind, index, signs, w, from_before, from_after):
    return pl.pallas_call(
        last_kernel,
        in_specs=[IN_SMEM] * 3 + [IN_VMEM] * 3,
        out_specs=IN_VMEM,
        out_shape=like(w.shape, BF16),
        compiler_params=params(),
        cost_estimate=cost(10**7, 3 * 10**6),
    )(kind, index, signs, w, from_before, from_after)


def body(multipliers, schur_inverse, corner_coupling, coarse_inverse, partner, corner_map):
    n_sub = lax.axis_size("sub")
    n_dom = lax.axis_size("dom")
    sub = lax.axis_index("sub")
    dom = lax.axis_index("dom")
    sub_dev, block_rows, rhs = multipliers.shape
    slots = block_rows // TILE
    coarse_block, coarse_dev = coarse_inverse.shape
    share = coarse_block // n_sub

    ids = sub * sub_dev + jnp.arange(sub_dev, dtype=jnp.int32)
    all_signs = jnp.where(ids[:, None] < partner, 1.0, -1.0).astype(F32)
    partners = lax.dynamic_slice_in_dim(partner, dom * slots, slots, 1)
    signs = lax.dynamic_slice_in_dim(all_signs, dom * slots, slots, 1)
    local = partners % sub_dev
    relation = (partners // sub_dev - sub) % n_sub
    kind = jnp.where(relation == 0, 0, jnp.where(relation == 1, 1, 2)).astype(jnp.int32)
    slot_ids = jnp.arange(slots, dtype=jnp.int32)[None]
    same_kind = kind[None] == kind[:, None]
    subs = jnp.arange(sub_dev, dtype=jnp.int32)
    earlier = same_kind & (subs[None] < subs[:, None])[:, :, None]
    lower = same_kind & (local[None] < local[:, None])
    sent = jnp.sum(earlier.astype(jnp.int32), axis=1) * slots + slot_ids
    got = jnp.sum(lower.astype(jnp.int32), axis=1) * slots + slot_ids
    after = jnp.where(kind == 1, sent, -1)
    before = jnp.where(kind == 2, sent, -1)
    index = jnp.where(kind == 0, local, got)

    corner_local = corner_map - sub * coarse_dev
    corner_table = (
        corner_local[:, :, None] == jnp.arange(coarse_dev, dtype=jnp.int32)[None, None]
    ).astype(BF16)
    coupling = jnp.einsum(
        "sjk,sjn->skn", corner_table, corner_coupling, preferred_element_type=F32
    ).astype(BF16)
    def own_rows(part):
        by_sub = lax.all_to_all(part.reshape(n_sub, share, rhs), "sub", 0, 0, tiled=True)
        return jnp.sum(by_sub.astype(F32), axis=0)

    far = swapped(multipliers, "dom", 2)
    near = swapped(multipliers, "dom", 1)
    near_far = swapped(far, "dom", 1)
    signed = coupling.reshape(sub_dev, coarse_dev, slots, TILE) * signs[:, None, :, None].astype(BF16)
    load1 = jnp.einsum(
        "skn,snr->kr", signed.reshape(coupling.shape), multipliers, preferred_element_type=F32
    )
    quarters = coarse_inverse.reshape(2, coarse_block // (2 * coarse_dev), n_dom, share, coarse_dev)
    quarters = quarters.transpose(2, 1, 3, 0, 4).reshape(n_dom, -1, 2 * coarse_dev)
    to_dom = jnp.concatenate(
        [quarters, jnp.broadcast_to(load1[None], (n_dom,) + load1.shape)], axis=1
    )
    inverse = lax.all_to_all(to_dom, "dom", 0, 0, tiled=True)
    part1 = first_part(inverse)
    across = packed_coupling(after, before, coupling)
    spread, second = spread_of(
        kind, index, coupling, shifted(across[0], "sub", 1), shifted(across[1], "sub", -1)
    )
    direct1, to_after, to_before = product(
        schur_inverse, (multipliers, near, far, near_far), (after, before, all_signs)
    )
    got_before, got_after = shifted(to_after, "sub", 1), shifted(to_before, "sub", -1)
    rows = own_rows(part1)
    rows1 = [shifted(rows, "sub", 1), rows, shifted(rows, "sub", -1)]
    got_before, got_after, rows1 = lax.optimization_barrier((got_before, got_after, rows1))
    delta1, sent1 = difference(
        kind, index, rows1, direct1, got_before, got_after, coupling, second
    )
    all1 = lax.all_gather(sent1, "dom", axis=0)

    u2, part2 = next_values(all1, delta1, spread, inverse, share)
    u2 = u2.reshape(multipliers.shape)
    far2 = swapped(u2, "dom", 2)
    near2 = swapped(u2, "dom", 1)
    own = own_rows(part2)
    near_far2 = swapped(far2, "dom", 1)
    near_far2, own = lax.optimization_barrier((near_far2, own))
    rows2 = [own] + [swapped(own, "dom", m) for m in range(1, n_dom)]
    (direct2,) = product(schur_inverse, (u2, near2, far2, near_far2))
    w2, to_after2, to_before2 = weighted(after, before, rows2, direct2, coupling)
    got_before2, got_after2 = shifted(to_after2, "sub", 1), shifted(to_before2, "sub", -1)
    result = last_values(kind, index, signs, w2, got_before2, got_after2)
    return result.reshape(sub_dev, block_rows, rhs)


def solution(mesh):
    placed = (
        P("sub", "dom", None),
        P("sub", "dom", None),
        P("sub", None, "dom"),
        P("dom", "sub"),
        P("sub", None),
        P("sub", None),
    )
    return jax.shard_map(
        body, mesh=mesh, in_specs=placed, out_specs=P("sub", "dom", None), check_vma=False
    )
```

```python
import functools

import jax
import jax.numpy as jnp
from jax import lax
from jax.experimental import pallas as pl
from jax.experimental.pallas import tpu as pltpu
from jax.sharding import PartitionSpec as P

TILE = 128
F32 = jnp.float32
BF16 = jnp.bfloat16
VMEM_BYTES = 24 * 1024 * 1024
MOST_VMEM_BYTES = 54 * 1024 * 1024
IN_SMEM = pl.BlockSpec(memory_space=pltpu.SMEM)
IN_VMEM = pl.BlockSpec(memory_space=pltpu.VMEM)


def like(shape, dtype):
    return jax.ShapeDtypeStruct(shape, dtype)


def params(limit=VMEM_BYTES):
    return pltpu.CompilerParams(vmem_limit_bytes=limit)


def cost(flops, moved):
    return pl.CostEstimate(flops=flops, bytes_accessed=moved, transcendentals=0)


def shifted(block, axis, distance):
    n = lax.axis_size(axis)
    return lax.ppermute(block, axis, [(i, (i + distance) % n) for i in range(n)])


def swapped(block, axis, mask):
    n = lax.axis_size(axis)
    return lax.ppermute(block, axis, [(i, i ^ mask) for i in range(n)])


def dot(a, b, dims=((1,), (0,))):
    return lax.dot_general(a, b, (dims, ((), ())), preferred_element_type=F32)


def split(x):
    high = x.astype(BF16)
    return high, (x - high.astype(F32)).astype(BF16)


def exact_dot(a, b):
    a_high, a_low = split(a)
    b_high, b_low = split(b)
    return dot(a_high, b_high) + (dot(a_high, b_low) + dot(a_low, b_high))


def applied(spread, high, low):
    return dot(spread, high, ((0,), (0,))) + dot(spread, low, ((0,), (0,)))


def partial_rows(got, load, part):
    height, half = got.shape[2], load.shape[0]
    for d in range(got.shape[0]):
        for h in range(2):
            at = (2 * d + h) * height
            block = got[d, :height, h * half : (h + 1) * half]
            part[at : at + height] = exact_dot(block, load).astype(BF16)


def first_kernel(got, part):
    height = got.shape[2]
    load = (got[0, height:] + got[1, height:]) + (got[2, height:] + got[3, height:])
    partial_rows(got, load, part)


def first_part(got):
    rows = 2 * got.shape[0] * got.shape[2]
    return pl.pallas_call(
        first_kernel,
        in_specs=[IN_VMEM],
        out_specs=IN_VMEM,
        out_shape=like((rows, got.shape[2]), BF16),
        compiler_params=params(),
        cost_estimate=cost(10**7, 10**6),
    )(got)


def pack_tiles(after, before, to_after, to_before, tile_at):
    sub_dev, slots = after.shape
    to_after[...] = jnp.zeros_like(to_after)
    to_before[...] = jnp.zeros_like(to_before)
    for i in range(sub_dev):
        for t in range(slots):
            for table, target in ((after, to_after), (before, to_before)):
                place = table[i, t]

                @pl.when(place >= 0)
                def _(i=i, t=t, place=place, target=target):
                    target[pl.ds(place, 1)] = tile_at(i, t).astype(BF16)[None]


def product_kernel(first, *refs):
    if first:
        after, before, signs, s_ref, u0, u1, u2, u3, coupling, direct_ref, to_after, to_before = refs
    else:
        s_ref, u0, u1, u2, u3, direct_ref = refs
    depth, rhs = u0.shape[1:]
    slots = direct_ref.shape[0]
    dom = lax.axis_index("dom")
    step = pl.program_id(0)
    total = None
    for m, piece in enumerate((u0, u1, u2, u3)):
        place = dom ^ m
        values = piece[0]
        if first:
            values = jnp.concatenate(
                [
                    (values[t * TILE : (t + 1) * TILE].astype(F32) * signs[step, place * slots + t]).astype(
                        BF16
                    )
                    for t in range(slots)
                ],
                axis=0,
            )
        columns = pl.ds(pl.multiple_of(place * depth, depth), depth)
        term = dot(s_ref[0, :, columns], values)
        total = term if total is None else total + term
    direct_ref[...] = total.reshape(slots, TILE, rhs)
    if first:

        @pl.when(step == 0)
        def _():
            to_after[...] = jnp.zeros_like(to_after)
            to_before[...] = jnp.zeros_like(to_before)

        for t in range(slots):
            for table, target in ((after, to_after), (before, to_before)):
                place = table[step, t]

                @pl.when(place >= 0)
                def _(t=t, place=place, target=target):
                    target[pl.ds(place, 1), :TILE] = direct_ref[pl.ds(t, 1)].astype(BF16)
                    target[pl.ds(place, 1), TILE:] = coupling[0:1, :, t * TILE : (t + 1) * TILE]


def product(schur_inverse, pieces, tables=(), coupling=None):
    sub_dev, rows, cols = schur_inverse.shape
    depth, rhs = pieces[0].shape[1:]
    slots = rows // TILE
    first = bool(tables)
    out_shape = [like((sub_dev * slots, TILE, rhs), F32)]
    out_specs = [pl.BlockSpec((slots, TILE, rhs), lambda i: (i, 0, 0))]
    if first:
        dofs = coupling.shape[1]
        packed = (2 * slots, TILE + dofs, rhs)
        out_shape += [like(packed, BF16)] * 2
        out_specs += [pl.BlockSpec(packed, lambda i: (0, 0, 0))] * 2
    return pl.pallas_call(
        functools.partial(product_kernel, first),
        grid=(sub_dev,),
        in_specs=[IN_SMEM] * len(tables)
        + [pl.BlockSpec((1, rows, cols), lambda i: (i, 0, 0))]
        + [pl.BlockSpec((1, depth, rhs), lambda i: (i, 0, 0))] * len(pieces)
        + ([pl.BlockSpec((1, dofs, rows), lambda i: (i, 0, 0))] if first else []),
        out_specs=out_specs,
        out_shape=out_shape,
        compiler_params=params(MOST_VMEM_BYTES),
        cost_estimate=cost(1000, 1000),
    )(*tables, schur_inverse, *pieces, *([coupling] if first else []))


def weighted_kernel(after, before, r0, r1, r2, r3, direct, coupling, w_ref, to_after, to_before, coarse):
    share = r0.shape[0]
    dom = lax.axis_index("dom")
    for m, rows in enumerate((r0, r1, r2, r3)):
        coarse[pl.ds(pl.multiple_of((dom ^ m) * share, share), share)] = rows[...]
    high, low = split(coarse[...])
    sub_dev = coupling.shape[0]
    slots = direct.shape[0] // sub_dev
    for i in range(sub_dev):
        for t in range(slots):
            own = coupling[i, :, t * TILE : (t + 1) * TILE]
            w_ref[i * slots + t] = (direct[i * slots + t] + applied(own, high, low)).astype(BF16)
    pack_tiles(after, before, to_after, to_before, lambda i, t: w_ref[i * slots + t])


def weighted(after, before, rows, direct, coupling):
    rhs = direct.shape[2]
    packed = (2 * after.shape[1], TILE, rhs)
    return pl.pallas_call(
        weighted_kernel,
        in_specs=[IN_SMEM] * 2 + [IN_VMEM] * 6,
        out_specs=[IN_VMEM] * 3,
        out_shape=[like(direct.shape, BF16), like(packed, BF16), like(packed, BF16)],
        scratch_shapes=[pltpu.VMEM((4 * rows[0].shape[0], rhs), F32)],
        compiler_params=params(),
        cost_estimate=cost(10**8, 3 * 10**6),
    )(after, before, *rows, direct, coupling)


def difference_kernel(kind, index, r0, r1, r2, direct, from_before, from_after, coupling, delta, spread, sent):
    sub_dev, dofs, _ = coupling.shape
    share = r0.shape[0]
    for b, rows in enumerate((r0, r1, r2)):
        sent[b * share : (b + 1) * share] = rows[...]
    at = 3 * share
    slots = kind.shape[1]
    blank = jnp.zeros((dofs, TILE), BF16)
    first, second = None, None
    for i in range(sub_dev):
        for t in range(slots):
            p = i * slots + t
            columns = slice(t * TILE, (t + 1) * TILE)
            mine = coupling[i, :, columns]
            where, which = kind[i, t], index[i, t]
            spread[p, :dofs] = blank
            spread[p, dofs : 2 * dofs] = mine
            spread[p, 2 * dofs :] = blank

            @pl.when(where == 0)
            def _(p=p, i=i, t=t, which=which, columns=columns):
                delta[p] = direct[p] - direct[which * slots + t]
                other = coupling[i, :, columns].astype(F32) - coupling[which, :, columns].astype(F32)
                spread[p, dofs : 2 * dofs] = other.astype(BF16)

            @pl.when(where == 1)
            def _(p=p, which=which):
                delta[p] = direct[p] - from_after[which, :TILE].astype(F32)
                spread[p, 2 * dofs :] = -from_after[which, TILE:]

            @pl.when(where == 2)
            def _(p=p, which=which):
                delta[p] = direct[p] - from_before[which, :TILE].astype(F32)
                spread[p, :dofs] = -from_before[which, TILE:]

            one = dot(mine, delta[p].astype(BF16))
            two = dot(mine, spread[p], ((1,), (1,)))
            first = one if first is None else first + one
            second = two if second is None else second + two
    sent[at : at + dofs] = first
    sent[at + dofs : at + 2 * dofs] = second[:, :TILE]
    sent[at + 2 * dofs :] = jnp.concatenate([second[:, TILE:], jnp.zeros_like(second[:, TILE:])], axis=1)


def difference(kind, index, rows, direct, from_before, from_after, coupling):
    n_tiles, _, rhs = direct.shape
    dofs = coupling.shape[1]
    return pl.pallas_call(
        difference_kernel,
        in_specs=[IN_SMEM] * 2 + [IN_VMEM] * 7,
        out_specs=[IN_VMEM] * 3,
        out_shape=[
            like(direct.shape, F32),
            like((n_tiles, 3 * dofs, TILE), BF16),
            like((3 * rows[0].shape[0] + 3 * dofs, rhs), F32),
        ],
        compiler_params=params(),
        cost_estimate=cost(10**8, 3 * 10**6),
    )(kind, index, *rows, direct, from_before, from_after, coupling)


def coarse_rows(got, share):
    return jnp.concatenate(
        [got[d, b * share : (b + 1) * share] for b in range(3) for d in range(got.shape[0])], axis=0
    )


def next_kernel(share, dofs, got, delta, spread, inverse, u_ref, part):
    coarse = coarse_rows(got, share)
    at = 3 * share
    total = (got[0, at:] + got[1, at:]) + (got[2, at:] + got[3, at:])
    load = total[:dofs] + exact_dot(total[dofs : 2 * dofs], coarse[:TILE])
    load = load + exact_dot(total[2 * dofs :, : 3 * dofs - TILE], coarse[TILE:])
    partial_rows(inverse, load, part)
    high, low = split(coarse)
    for p in range(delta.shape[0]):
        u_ref[p] = (delta[p] + applied(spread[p], high, low)).astype(BF16)


def next_values(got, delta, spread, inverse, share):
    dofs = spread.shape[1] // 3
    rhs = delta.shape[2]
    part = (2 * inverse.shape[0] * inverse.shape[2], rhs)
    return pl.pallas_call(
        functools.partial(next_kernel, share, dofs),
        in_specs=[IN_VMEM] * 4,
        out_specs=[IN_VMEM] * 2,
        out_shape=[like(delta.shape, BF16), like(part, BF16)],
        compiler_params=params(),
        cost_estimate=cost(10**8, 3 * 10**6),
    )(got, delta, spread, inverse)


def last_kernel(kind, index, signs, w, from_before, from_after, out):
    sub_dev, slots = kind.shape
    for i in range(sub_dev):
        for t in range(slots):
            p = i * slots + t
            where, which = kind[i, t], index[i, t]

            def put(tile, p=p, i=i, t=t):
                out[p] = (signs[i, t] * (w[p].astype(F32) - tile.astype(F32))).astype(BF16)

            @pl.when(where == 0)
            def _(put=put, which=which, t=t):
                put(w[which * slots + t])

            @pl.when(where == 1)
            def _(put=put, which=which):
                put(from_after[which])

            @pl.when(where == 2)
            def _(put=put, which=which):
                put(from_before[which])


def last_values(kind, index, signs, w, from_before, from_after):
    return pl.pallas_call(
        last_kernel,
        in_specs=[IN_SMEM] * 3 + [IN_VMEM] * 3,
        out_specs=IN_VMEM,
        out_shape=like(w.shape, BF16),
        compiler_params=params(),
        cost_estimate=cost(10**7, 3 * 10**6),
    )(kind, index, signs, w, from_before, from_after)


def body(multipliers, schur_inverse, corner_coupling, coarse_inverse, partner, corner_map):
    n_sub = lax.axis_size("sub")
    n_dom = lax.axis_size("dom")
    sub = lax.axis_index("sub")
    dom = lax.axis_index("dom")
    sub_dev, block_rows, rhs = multipliers.shape
    slots = block_rows // TILE
    coarse_block, coarse_dev = coarse_inverse.shape
    share = coarse_block // n_sub

    ids = sub * sub_dev + jnp.arange(sub_dev, dtype=jnp.int32)
    all_signs = jnp.where(ids[:, None] < partner, 1.0, -1.0).astype(F32)
    partners = lax.dynamic_slice_in_dim(partner, dom * slots, slots, 1)
    signs = lax.dynamic_slice_in_dim(all_signs, dom * slots, slots, 1)
    local = partners % sub_dev
    relation = (partners // sub_dev - sub) % n_sub
    kind = jnp.where(relation == 0, 0, jnp.where(relation == 1, 1, 2)).astype(jnp.int32)
    slot_ids = jnp.arange(slots, dtype=jnp.int32)[None]
    same_kind = kind[None] == kind[:, None]
    subs = jnp.arange(sub_dev, dtype=jnp.int32)
    earlier = same_kind & (subs[None] < subs[:, None])[:, :, None]
    lower = same_kind & (local[None] < local[:, None])
    sent = jnp.sum(earlier.astype(jnp.int32), axis=1) * slots + slot_ids
    got = jnp.sum(lower.astype(jnp.int32), axis=1) * slots + slot_ids
    after = jnp.where(kind == 1, sent, -1)
    before = jnp.where(kind == 2, sent, -1)
    index = jnp.where(kind == 0, local, got)

    corner_local = corner_map - sub * coarse_dev
    corner_table = (
        corner_local[:, :, None] == jnp.arange(coarse_dev, dtype=jnp.int32)[None, None]
    ).astype(BF16)
    coupling = jnp.einsum(
        "sjk,sjn->skn", corner_table, corner_coupling, preferred_element_type=F32
    ).astype(BF16)
    def by_sub(part):
        return lax.all_to_all(part.reshape(n_sub, share, rhs), "sub", 0, 0, tiled=True)

    def summed(blocks):
        return jnp.sum(blocks.astype(F32), axis=0)

    far = swapped(multipliers, "dom", 2)
    near = swapped(multipliers, "dom", 1)
    near_far = swapped(far, "dom", 1)
    signed = coupling.reshape(sub_dev, coarse_dev, slots, TILE) * signs[:, None, :, None].astype(BF16)
    load1 = jnp.einsum(
        "skn,snr->kr", signed.reshape(coupling.shape), multipliers, preferred_element_type=F32
    )
    quarters = coarse_inverse.reshape(2, coarse_block // (2 * coarse_dev), n_dom, share, coarse_dev)
    quarters = quarters.transpose(2, 1, 3, 0, 4).reshape(n_dom, -1, 2 * coarse_dev)
    to_dom = jnp.concatenate(
        [quarters, jnp.broadcast_to(load1[None], (n_dom,) + load1.shape)], axis=1
    )
    inverse = lax.all_to_all(to_dom, "dom", 0, 0, tiled=True)
    part1 = first_part(inverse)
    direct1, to_after, to_before = product(
        schur_inverse, (multipliers, near, far, near_far), (after, before, all_signs), coupling
    )
    got_before, got_after = shifted(to_after, "sub", 1), shifted(to_before, "sub", -1)
    rows = summed(by_sub(part1))
    rows1 = [shifted(rows, "sub", 1), rows, shifted(rows, "sub", -1)]
    got_before, got_after, rows1 = lax.optimization_barrier((got_before, got_after, rows1))
    delta1, spread, sent1 = difference(kind, index, rows1, direct1, got_before, got_after, coupling)
    all1 = lax.all_gather(sent1, "dom", axis=0)

    u2, part2 = next_values(all1, delta1, spread, inverse, share)
    u2 = u2.reshape(multipliers.shape)
    far2 = swapped(u2, "dom", 2)
    near2 = swapped(u2, "dom", 1)
    near_far2 = jnp.concatenate(
        [swapped(far2[i : i + 1], "dom", 1) for i in range(sub_dev)], axis=0
    )
    (direct2,) = product(schur_inverse, (u2, near2, far2, near_far2))
    by_sub2, direct2 = lax.optimization_barrier((by_sub(part2), direct2))
    own = summed(by_sub2)
    rows2 = [own] + [swapped(own, "dom", m) for m in range(1, n_dom)]
    w2, to_after2, to_before2 = weighted(after, before, rows2, direct2, coupling)
    got_before2, got_after2 = shifted(to_after2, "sub", 1), shifted(to_before2, "sub", -1)
    result = last_values(kind, index, signs, w2, got_before2, got_after2)
    return result.reshape(sub_dev, block_rows, rhs)


def solution(mesh):
    placed = (
        P("sub", "dom", None),
        P("sub", "dom", None),
        P("sub", None, "dom"),
        P("dom", "sub"),
        P("sub", None),
        P("sub", None),
    )
    return jax.shard_map(
        body, mesh=mesh, in_specs=placed, out_specs=P("sub", "dom", None), check_vma=False
    )
```

```python
import functools

import jax
import jax.numpy as jnp
from jax import lax
from jax.experimental import pallas as pl
from jax.experimental.pallas import tpu as pltpu
from jax.sharding import PartitionSpec as P

TILE = 128
F32 = jnp.float32
BF16 = jnp.bfloat16
VMEM_BYTES = 24 * 1024 * 1024
MOST_VMEM_BYTES = 54 * 1024 * 1024
IN_SMEM = pl.BlockSpec(memory_space=pltpu.SMEM)
IN_VMEM = pl.BlockSpec(memory_space=pltpu.VMEM)
IN_HBM = pl.BlockSpec(memory_space=pltpu.HBM)


def like(shape, dtype):
    return jax.ShapeDtypeStruct(shape, dtype)


def params(limit=VMEM_BYTES):
    return pltpu.CompilerParams(vmem_limit_bytes=limit)


def cost(flops, moved):
    return pl.CostEstimate(flops=flops, bytes_accessed=moved, transcendentals=0)


def shifted(block, axis, distance):
    n = lax.axis_size(axis)
    return lax.ppermute(block, axis, [(i, (i + distance) % n) for i in range(n)])


def swapped(block, axis, mask):
    n = lax.axis_size(axis)
    return lax.ppermute(block, axis, [(i, i ^ mask) for i in range(n)])


def dot(a, b, dims=((1,), (0,))):
    return lax.dot_general(a, b, (dims, ((), ())), preferred_element_type=F32)


def split(x):
    high = x.astype(BF16)
    return high, (x - high.astype(F32)).astype(BF16)


def exact_dot(a, b):
    a_high, a_low = split(a)
    b_high, b_low = split(b)
    return dot(a_high, b_high) + (dot(a_high, b_low) + dot(a_low, b_high))


def applied(spread, high, low):
    return dot(spread, high, ((0,), (0,))) + dot(spread, low, ((0,), (0,)))


def partial_rows(got, load, part):
    height, half = got.shape[2], load.shape[0]
    for d in range(got.shape[0]):
        for h in range(2):
            at = (2 * d + h) * height
            block = got[d, :height, h * half : (h + 1) * half]
            part[at : at + height] = exact_dot(block, load).astype(BF16)


def first_kernel(got, part):
    height = got.shape[2]
    load = (got[0, height:] + got[1, height:]) + (got[2, height:] + got[3, height:])
    partial_rows(got, load, part)


def first_part(got):
    rows = 2 * got.shape[0] * got.shape[2]
    return pl.pallas_call(
        first_kernel,
        in_specs=[IN_VMEM],
        out_specs=IN_VMEM,
        out_shape=like((rows, got.shape[2]), BF16),
        compiler_params=params(),
        cost_estimate=cost(10**7, 10**6),
    )(got)


def pack_tiles(after, before, to_after, to_before, tile_at):
    sub_dev, slots = after.shape
    to_after[...] = jnp.zeros_like(to_after)
    to_before[...] = jnp.zeros_like(to_before)
    for i in range(sub_dev):
        for t in range(slots):
            for table, target in ((after, to_after), (before, to_before)):
                place = table[i, t]

                @pl.when(place >= 0)
                def _(i=i, t=t, place=place, target=target):
                    target[pl.ds(place, 1)] = tile_at(i, t).astype(BF16)[None]


def product_kernel(first, *refs):
    if first:
        after, before, signs, s_ref, u0, u1, u2, u3, coupling, direct_ref, to_after, to_before = refs
    else:
        s_ref, u0, u1, u2, u3, direct_ref = refs
    depth, rhs = u0.shape[1:]
    slots = direct_ref.shape[0]
    dom = lax.axis_index("dom")
    step = pl.program_id(0)
    total = None
    for m, piece in enumerate((u0, u1, u2, u3)):
        place = dom ^ m
        values = piece[0]
        if first:
            values = jnp.concatenate(
                [
                    (values[t * TILE : (t + 1) * TILE].astype(F32) * signs[step, place * slots + t]).astype(
                        BF16
                    )
                    for t in range(slots)
                ],
                axis=0,
            )
        columns = pl.ds(pl.multiple_of(place * depth, depth), depth)
        term = dot(s_ref[0, :, columns], values)
        total = term if total is None else total + term
    direct_ref[...] = total.reshape(slots, TILE, rhs)
    if first:

        @pl.when(step == 0)
        def _():
            to_after[...] = jnp.zeros_like(to_after)
            to_before[...] = jnp.zeros_like(to_before)

        for t in range(slots):
            for table, target in ((after, to_after), (before, to_before)):
                place = table[step, t]

                @pl.when(place >= 0)
                def _(t=t, place=place, target=target):
                    target[pl.ds(place, 1), :TILE] = direct_ref[pl.ds(t, 1)].astype(BF16)
                    target[pl.ds(place, 1), TILE:] = coupling[0:1, :, t * TILE : (t + 1) * TILE]


def product(schur_inverse, pieces, tables=(), coupling=None):
    sub_dev, rows, cols = schur_inverse.shape
    depth, rhs = pieces[0].shape[1:]
    slots = rows // TILE
    first = bool(tables)
    out_shape = [like((sub_dev * slots, TILE, rhs), F32)]
    out_specs = [pl.BlockSpec((slots, TILE, rhs), lambda i: (i, 0, 0))]
    if first:
        dofs = coupling.shape[1]
        packed = (2 * slots, TILE + dofs, rhs)
        out_shape += [like(packed, BF16)] * 2
        out_specs += [pl.BlockSpec(packed, lambda i: (0, 0, 0))] * 2
    return pl.pallas_call(
        functools.partial(product_kernel, first),
        grid=(sub_dev,),
        in_specs=[IN_SMEM] * len(tables)
        + [pl.BlockSpec((1, rows, cols), lambda i: (i, 0, 0))]
        + [pl.BlockSpec((1, depth, rhs), lambda i: (i, 0, 0))] * len(pieces)
        + ([pl.BlockSpec((1, dofs, rows), lambda i: (i, 0, 0))] if first else []),
        out_specs=out_specs,
        out_shape=out_shape,
        compiler_params=params(MOST_VMEM_BYTES),
        cost_estimate=cost(1000, 1000),
    )(*tables, schur_inverse, *pieces, *([coupling] if first else []))


def weighted_kernel(
    after, before, r0, r1, r2, r3, direct_in, coupling, w_ref, to_after, to_before, coarse, direct, sem
):
    fetch = pltpu.make_async_copy(direct_in, direct, sem.at[0])
    fetch.start()
    share = r0.shape[0]
    dom = lax.axis_index("dom")
    for m, rows in enumerate((r0, r1, r2, r3)):
        coarse[pl.ds(pl.multiple_of((dom ^ m) * share, share), share)] = rows[...]
    high, low = split(coarse[...])
    sub_dev = coupling.shape[0]
    slots = direct.shape[0] // sub_dev
    fetch.wait()
    for i in range(sub_dev):
        for t in range(slots):
            own = coupling[i, :, t * TILE : (t + 1) * TILE]
            w_ref[i * slots + t] = (direct[i * slots + t] + applied(own, high, low)).astype(BF16)
    pack_tiles(after, before, to_after, to_before, lambda i, t: w_ref[i * slots + t])


def weighted(after, before, rows, direct, coupling):
    rhs = direct.shape[2]
    packed = (2 * after.shape[1], TILE, rhs)
    return pl.pallas_call(
        weighted_kernel,
        in_specs=[IN_SMEM] * 2 + [IN_VMEM] * 4 + [IN_HBM, IN_VMEM],
        out_specs=[IN_VMEM] * 3,
        out_shape=[like(direct.shape, BF16), like(packed, BF16), like(packed, BF16)],
        scratch_shapes=[
            pltpu.VMEM((4 * rows[0].shape[0], rhs), F32),
            pltpu.VMEM(direct.shape, F32),
            pltpu.SemaphoreType.DMA((1,)),
        ],
        compiler_params=params(),
        cost_estimate=cost(10**8, 3 * 10**6),
    )(after, before, *rows, direct, coupling)


def difference_kernel(
    kind, index, r0, r1, r2, direct_in, from_before, from_after, coupling, delta, spread, sent, direct, sem
):
    fetch = pltpu.make_async_copy(direct_in, direct, sem.at[0])
    fetch.start()
    sub_dev, dofs, _ = coupling.shape
    share = r0.shape[0]
    for b, rows in enumerate((r0, r1, r2)):
        sent[b * share : (b + 1) * share] = rows[...]
    at = 3 * share
    slots = kind.shape[1]
    blank = jnp.zeros((dofs, TILE), BF16)
    first, second = None, None
    for i in range(sub_dev):
        for t in range(slots):
            p = i * slots + t
            columns = slice(t * TILE, (t + 1) * TILE)
            mine = coupling[i, :, columns]
            where, which = kind[i, t], index[i, t]
            spread[p, :dofs] = blank
            spread[p, dofs : 2 * dofs] = mine
            spread[p, 2 * dofs :] = blank

            @pl.when(where == 0)
            def _(p=p, i=i, which=which, columns=columns):
                other = coupling[i, :, columns].astype(F32) - coupling[which, :, columns].astype(F32)
                spread[p, dofs : 2 * dofs] = other.astype(BF16)

            @pl.when(where == 1)
            def _(p=p, which=which):
                spread[p, 2 * dofs :] = -from_after[which, TILE:]

            @pl.when(where == 2)
            def _(p=p, which=which):
                spread[p, :dofs] = -from_before[which, TILE:]

            two = dot(mine, spread[p], ((1,), (1,)))
            second = two if second is None else second + two
    sent[at + dofs : at + 2 * dofs] = second[:, :TILE]
    rest = second[:, TILE:]
    sent[at + 2 * dofs :] = jnp.concatenate([rest[: dofs // 2], rest[dofs // 2 :]], axis=1)
    fetch.wait()
    for i in range(sub_dev):
        for t in range(slots):
            p = i * slots + t
            other = chosen(
                kind[i, t],
                index[i, t],
                lambda j, t=t: direct[j * slots + t],
                lambda j: from_after[j, :TILE],
                lambda j: from_before[j, :TILE],
            )
            value = direct[p] - other
            delta[p] = value
            one = dot(coupling[i, :, t * TILE : (t + 1) * TILE], value.astype(BF16))
            first = one if first is None else first + one
    sent[at : at + dofs] = first


def difference(kind, index, rows, direct, from_before, from_after, coupling):
    n_tiles, _, rhs = direct.shape
    dofs = coupling.shape[1]
    return pl.pallas_call(
        difference_kernel,
        in_specs=[IN_SMEM] * 2 + [IN_VMEM] * 3 + [IN_HBM] + [IN_VMEM] * 3,
        out_specs=[IN_VMEM] * 3,
        out_shape=[
            like(direct.shape, F32),
            like((n_tiles, 3 * dofs, TILE), BF16),
            like((3 * rows[0].shape[0] + 2 * dofs + dofs // 2, rhs), F32),
        ],
        scratch_shapes=[pltpu.VMEM(direct.shape, F32), pltpu.SemaphoreType.DMA((1,))],
        compiler_params=params(),
        cost_estimate=cost(10**8, 3 * 10**6),
    )(kind, index, *rows, direct, from_before, from_after, coupling)


def coarse_rows(got, share):
    return jnp.concatenate(
        [got[d, b * share : (b + 1) * share] for b in range(3) for d in range(got.shape[0])], axis=0
    )


def next_kernel(share, dofs, got, delta, spread, inverse, u_ref, part):
    coarse = coarse_rows(got, share)
    at = 3 * share
    total = (got[0, at:] + got[1, at:]) + (got[2, at:] + got[3, at:])
    load = total[:dofs] + exact_dot(total[dofs : 2 * dofs], coarse[:TILE])
    rest = total[2 * dofs :]
    rest = jnp.concatenate([rest[:, :dofs], rest[:, dofs:]], axis=0)
    load = load + exact_dot(rest, coarse[TILE:])
    partial_rows(inverse, load, part)
    high, low = split(coarse)
    for p in range(delta.shape[0]):
        u_ref[p] = (delta[p] + applied(spread[p], high, low)).astype(BF16)


def next_values(got, delta, spread, inverse, share):
    dofs = spread.shape[1] // 3
    rhs = delta.shape[2]
    part = (2 * inverse.shape[0] * inverse.shape[2], rhs)
    return pl.pallas_call(
        functools.partial(next_kernel, share, dofs),
        in_specs=[IN_VMEM] * 4,
        out_specs=[IN_VMEM] * 2,
        out_shape=[like(delta.shape, BF16), like(part, BF16)],
        compiler_params=params(),
        cost_estimate=cost(10**8, 3 * 10**6),
    )(got, delta, spread, inverse)


def chosen(where, which, own, from_after, from_before):
    after = from_after(jnp.where(where == 1, which, 0)).astype(F32)
    before = from_before(jnp.where(where == 2, which, 0)).astype(F32)
    return jnp.where(where == 0, own(jnp.where(where == 0, which, 0)).astype(F32), jnp.where(where == 1, after, before))


def last_kernel(kind, index, signs, w, from_before, from_after, out):
    sub_dev, slots = kind.shape
    for i in range(sub_dev):
        for t in range(slots):
            p = i * slots + t
            other = chosen(
                kind[i, t],
                index[i, t],
                lambda j, t=t: w[j * slots + t],
                lambda j: from_after[j],
                lambda j: from_before[j],
            )
            out[p] = (signs[i, t] * (w[p].astype(F32) - other)).astype(BF16)


def last_values(kind, index, signs, w, from_before, from_after):
    return pl.pallas_call(
        last_kernel,
        in_specs=[IN_SMEM] * 3 + [IN_VMEM] * 3,
        out_specs=IN_VMEM,
        out_shape=like(w.shape, BF16),
        compiler_params=params(),
        cost_estimate=cost(10**7, 3 * 10**6),
    )(kind, index, signs, w, from_before, from_after)


def body(multipliers, schur_inverse, corner_coupling, coarse_inverse, partner, corner_map):
    n_sub = lax.axis_size("sub")
    n_dom = lax.axis_size("dom")
    sub = lax.axis_index("sub")
    dom = lax.axis_index("dom")
    sub_dev, block_rows, rhs = multipliers.shape
    slots = block_rows // TILE
    coarse_block, coarse_dev = coarse_inverse.shape
    share = coarse_block // n_sub

    ids = sub * sub_dev + jnp.arange(sub_dev, dtype=jnp.int32)
    all_signs = jnp.where(ids[:, None] < partner, 1.0, -1.0).astype(F32)
    partners = lax.dynamic_slice_in_dim(partner, dom * slots, slots, 1)
    signs = lax.dynamic_slice_in_dim(all_signs, dom * slots, slots, 1)
    local = partners % sub_dev
    relation = (partners // sub_dev - sub) % n_sub
    kind = jnp.where(relation == 0, 0, jnp.where(relation == 1, 1, 2)).astype(jnp.int32)
    slot_ids = jnp.arange(slots, dtype=jnp.int32)[None]
    same_kind = kind[None] == kind[:, None]
    subs = jnp.arange(sub_dev, dtype=jnp.int32)
    earlier = same_kind & (subs[None] < subs[:, None])[:, :, None]
    lower = same_kind & (local[None] < local[:, None])
    sent = jnp.sum(earlier.astype(jnp.int32), axis=1) * slots + slot_ids
    got = jnp.sum(lower.astype(jnp.int32), axis=1) * slots + slot_ids
    after = jnp.where(kind == 1, sent, -1)
    before = jnp.where(kind == 2, sent, -1)
    index = jnp.where(kind == 0, local, got)

    corner_local = corner_map - sub * coarse_dev
    corner_table = (
        corner_local[:, :, None] == jnp.arange(coarse_dev, dtype=jnp.int32)[None, None]
    ).astype(BF16)
    coupling = jnp.einsum(
        "sjk,sjn->skn", corner_table, corner_coupling, preferred_element_type=F32
    ).astype(BF16)
    def by_sub(part):
        return lax.all_to_all(part.reshape(n_sub, share, rhs), "sub", 0, 0, tiled=True)

    def summed(blocks):
        return jnp.sum(blocks.astype(F32), axis=0)

    far = swapped(multipliers, "dom", 2)
    near = swapped(multipliers, "dom", 1)
    near_far = swapped(far, "dom", 1)
    signed = coupling.reshape(sub_dev, coarse_dev, slots, TILE) * signs[:, None, :, None].astype(BF16)
    load1 = jnp.einsum(
        "skn,snr->kr", signed.reshape(coupling.shape), multipliers, preferred_element_type=F32
    )
    quarters = coarse_inverse.reshape(2, coarse_block // (2 * coarse_dev), n_dom, share, coarse_dev)
    quarters = quarters.transpose(2, 1, 3, 0, 4).reshape(n_dom, -1, 2 * coarse_dev)
    to_dom = jnp.concatenate(
        [quarters, jnp.broadcast_to(load1[None], (n_dom,) + load1.shape)], axis=1
    )
    inverse = lax.all_to_all(to_dom, "dom", 0, 0, tiled=True)
    part1 = first_part(inverse)
    direct1, to_after, to_before = product(
        schur_inverse, (multipliers, near, far, near_far), (after, before, all_signs), coupling
    )
    got_before, got_after = shifted(to_after, "sub", 1), shifted(to_before, "sub", -1)
    rows = summed(by_sub(part1))
    rows1 = [shifted(rows, "sub", 1), rows, shifted(rows, "sub", -1)]
    got_before, got_after, rows1 = lax.optimization_barrier((got_before, got_after, rows1))
    delta1, spread, sent1 = difference(kind, index, rows1, direct1, got_before, got_after, coupling)
    all1 = lax.all_gather(sent1, "dom", axis=0)

    u2, part2 = next_values(all1, delta1, spread, inverse, share)
    u2 = u2.reshape(multipliers.shape)
    far2 = swapped(u2, "dom", 2)
    near2 = swapped(u2, "dom", 1)
    near_far2 = jnp.concatenate(
        [swapped(far2[i : i + 1], "dom", 1) for i in range(sub_dev)], axis=0
    )
    (direct2,) = product(schur_inverse, (u2, near2, far2, near_far2))
    by_sub2, direct2 = lax.optimization_barrier((by_sub(part2), direct2))
    own = summed(by_sub2)
    rows2 = [own] + [swapped(own, "dom", m) for m in range(1, n_dom)]
    w2, to_after2, to_before2 = weighted(after, before, rows2, direct2, coupling)
    got_before2, got_after2 = shifted(to_after2, "sub", 1), shifted(to_before2, "sub", -1)
    result = last_values(kind, index, signs, w2, got_before2, got_after2)
    return result.reshape(sub_dev, block_rows, rhs)


def solution(mesh):
    placed = (
        P("sub", "dom", None),
        P("sub", "dom", None),
        P("sub", None, "dom"),
        P("dom", "sub"),
        P("sub", None),
        P("sub", None),
    )
    return jax.shard_map(
        body, mesh=mesh, in_specs=placed, out_specs=P("sub", "dom", None), check_vma=False
    )
```
